32 devices in a mesh: dp: 4 (over x, core), expert: 8 (over z, y).
Axes of the slice: x: 2, y: 2, z: 4, core: 2. Of those that a mesh axis runs over, the one named last changes fastest.
Arguments:
- out_grad: bfloat16 [4096, 2048], P(('dp', 'expert')), may hold values from -6 to 6
- combine: bfloat16 [4096, 6], P(('dp', 'expert')), may hold values from 0.049804688 to 0.59765625
- expert_ids: int32 [4096, 6], P(('dp', 'expert')), may hold values from 0 to 7, all different within a row; in each aligned block of 128 rows (0 to 127, 128 to 255, ...) at most 128 rows name the same one
- hidden: bfloat16 [8, 32, 128, 1408], P('expert', 'dp'), may hold values from -0.59765625 to 0.59765625
- w_down: bfloat16 [8, 2048, 1408], P('expert'), may hold values from -0.15625 to 0.15625
Outputs:
- grad_hidden: bfloat16 [8, 32, 128, 1408], P('expert', 'dp')
- grad_down: bfloat16 [8, 2048, 1408], P('expert', 'dp')
- grad_probs: float32 [4096, 6], P(('dp', 'expert'))
The draws below stay inside these ranges and needn't reach their ends.
Inputs may be any that keep to these rules, and one draw needn't show every extreme that they name: `expert_ids`: each row names 6 different experts. Among the 128 rows of one source device no expert is named more than 128 times, and in every draw some expert is named exactly 128 times by the rows of some device.
All inputs are finite; a program needn't handle non-finite values.
Results may differ from the reference program's by a relative error of at most 0.013.
Values may be sent and summed in bfloat16 or wider, within the bound.
No kernel may reach another device: no remote copies, remote signals or barrier semaphores. Data moves between devices by JAX's collectives and lax.ppermute only.
A program may use at most 64 MiB of HBM per device.

```python
import math
import jax
import jax.numpy as jnp
import numpy as np
from jax import lax

D = 2048
FF = 1408
TOP = 6
TOK_DEV = 128
REPLICAS = 4
GROUP = 8
SOURCES = 32
TOKENS = 4096
EXPERTS = 8
CAP = 128


def steps_of(stream_key, dims, split, low, largest):
    def one(axis_at, shards_of):
        draws = jax.random.uniform(jax.random.fold_in(jax.random.fold_in(stream_key, 6), axis_at), (shards_of,), jnp.float32, low / len(split), largest / len(split))
        return jnp.repeat(jnp.exp(draws), dims[axis_at] // shards_of).reshape((-1,) + (1,) * (len(dims) - axis_at - 1))

    level = one(*split[0])
    for cut in split[1:]:
        level = level * one(*cut)
    return level


def deal_out(stream_key, own, number, rows, count, top, most, slope):
    sequence = jax.random.permutation(stream_key, count)
    crowded, usual = shares(count, rows * top, most, slope, True), shares(count, rows * top, most, slope, False)
    places = jnp.arange(count)

    def named(lengths, turn):
        used = int((lengths > 0).sum())
        fixed = max(1, used // 4)
        moved = fixed + (places - fixed + turn * (used - fixed)) % max(1, count - fixed)
        return jnp.zeros((count,), jnp.int32).at[sequence[jnp.where(places < fixed, places, moved)]].set(jnp.asarray(lengths, jnp.int32))

    lengths = jnp.where(number % 4 == 0, named(crowded, number // 4), named(usual, number - number // 4 - 1))
    mixed = jax.random.permutation(jax.random.fold_in(own, 3), count)
    donor, taker = mixed[0:count // 2 * 2:2], mixed[1:count // 2 * 2:2]
    room = jnp.minimum(lengths[donor] - 1, most - lengths[taker]) // 2
    room = jnp.where((donor == sequence[0]) | (taker == sequence[0]) | (lengths[taker] == 0), 0, jnp.maximum(room, 0))
    moved = jax.random.randint(jax.random.fold_in(own, 4), (count // 2,), 0, 1 << 20) % (room + 1)
    lengths = lengths.at[donor].add(-moved).at[taker].add(moved)
    items = jnp.searchsorted(jnp.cumsum(lengths), jnp.arange(rows * top), side="right").astype(jnp.int32)
    listing = items.reshape(top, rows).T
    listing = listing[jax.random.permutation(jax.random.fold_in(own, 1), rows)]
    turn = jax.random.randint(jax.random.fold_in(own, 2), (rows, 1), 0, top)
    return jnp.take_along_axis(listing, (jnp.arange(top)[None, :] + turn) % top, axis=1)


def shares(count, total, limit, lean, full):
    loads = [(1 << 20) // math.isqrt(grade ** lean) + 1 for grade in range(1, count + 1)]
    largest = limit if full else min(limit, max(-(-total // count), total * loads[0] // sum(loads)))
    least = 1 if total - largest >= count - 1 else 0
    given, surplus = [largest] + [least] * (count - 1), total - largest - least * (count - 1)
    while surplus > 0:
        movable = [i for i in range(1, count) if given[i] < largest] or [i for i in range(1, count) if given[i] < limit]
        whole, left = sum([loads[i] for i in movable]), surplus
        for i in movable:
            more = min(limit - given[i], max(1, left * loads[i] // whole), surplus)
            given[i] = given[i] + more
            surplus = surplus - more
    return np.array(given)


def gaussian(rng, extent, scale, bound, cuts=(), kind=jnp.bfloat16):
    array = scale * jax.random.normal(rng, extent, jnp.float32)
    if cuts:
        array = array * steps_of(rng, extent, cuts, -0.22, 0.18)
    return jnp.clip(array, -bound, bound).astype(kind)


def setup_inputs(seed: int = 0) -> dict:
    key_list = jax.random.split(jax.random.key(seed), 6)
    out_grad = gaussian(key_list[0], (TOKENS, D), 1.0, 6.0, ((0, 32),))
    combine = jnp.clip(jnp.exp(math.log(0.59765625) - 2.4849066 * jax.random.uniform(key_list[1], (TOKENS, TOP), jnp.float32) ** steps_of(key_list[1], (TOKENS, TOP), ((0, 32),), -0.2, 0.2)), 0.049804688, 0.59765625).astype(jnp.bfloat16)
    expert_ids_keys = jax.random.split(jax.random.fold_in(key_list[2], 1), TOKENS // TOK_DEV)
    expert_ids_turns = jax.random.permutation(jax.random.fold_in(key_list[2], 3), TOKENS // TOK_DEV)
    expert_ids = jax.vmap(lambda own, number: deal_out(jax.random.fold_in(key_list[2], 2), own, number, TOK_DEV, EXPERTS, TOP, CAP, 2))(expert_ids_keys, expert_ids_turns).reshape((TOKENS, TOP))
    hidden = gaussian(key_list[3], (EXPERTS, SOURCES, CAP, FF), 0.1, 0.59765625, ((0, 8), (1, 4)))
    w_down = gaussian(key_list[4], (EXPERTS, D, FF), FF ** -0.5, 0.15625, ((0, 8),))
    return {"out_grad": out_grad, "combine": combine, "expert_ids": expert_ids, "hidden": hidden, "w_down": w_down}


def reference(out_grad, combine, expert_ids, hidden, w_down):
    pair_total = TOKENS * TOP
    chosen_grid = expert_ids.reshape(SOURCES, TOK_DEV * TOP)
    onehot = (chosen_grid[:, :, None] == jnp.arange(EXPERTS, dtype=jnp.int32)[None, None, :]).astype(jnp.int32)
    before = jnp.cumsum(onehot, axis=1) - onehot
    slot_rank = jnp.sum(before * onehot, axis=2).reshape(-1).astype(jnp.int32)
    source = (jnp.arange(pair_total, dtype=jnp.int32) // (TOK_DEV * TOP)).astype(jnp.int32)
    chosen = expert_ids.reshape(-1).astype(jnp.int32)
    bucket_pos = ((chosen * SOURCES + source) * CAP + slot_rank).astype(jnp.int32)
    pair_of = jnp.full((EXPERTS * SOURCES * CAP,), pair_total, jnp.int32)
    pair_of = pair_of.at[bucket_pos].set(jnp.arange(pair_total, dtype=jnp.int32))
    token_of = jnp.where(pair_of < pair_total, pair_of // TOP, TOKENS).astype(jnp.int32)
    grad_rows = jnp.concatenate([out_grad, jnp.zeros((1, D), out_grad.dtype)], axis=0)
    prob_rows = jnp.concatenate([combine.reshape(-1), jnp.zeros((1,), combine.dtype)], axis=0)
    token_table = token_of.reshape(EXPERTS, SOURCES * CAP)
    pair_table = pair_of.reshape(EXPERTS, SOURCES * CAP)

    def per_expert(packed):
        token_idx, pair_idx, saved, weight = packed
        slot_rows = grad_rows[token_idx]
        slot_prob = prob_rows[pair_idx].astype(jnp.float32)[:, None]
        saved_rows = saved.reshape(SOURCES * CAP, FF)
        projected = jnp.dot(slot_rows, weight, preferred_element_type=jnp.float32)
        hidden_grad = (slot_prob * projected).astype(jnp.bfloat16)
        slot_grad = jnp.sum(projected * saved_rows.astype(jnp.float32), axis=1)
        scaled = (slot_prob * slot_rows.astype(jnp.float32)).astype(jnp.bfloat16)
        partial_value = jnp.einsum("rnd,rnf->rdf",
                             scaled.reshape(REPLICAS, GROUP * CAP, D).astype(jnp.float32),
                             saved_rows.reshape(REPLICAS, GROUP * CAP, FF).astype(jnp.float32))
        partial_value = lax.optimization_barrier(partial_value.astype(jnp.bfloat16))
        down_grad = jnp.sum(partial_value.astype(jnp.float32), axis=0).astype(jnp.bfloat16)
        return hidden_grad.reshape(SOURCES, CAP, FF), slot_grad, down_grad

    grad_hidden, slot_grads, grad_down = lax.map(per_expert, (token_table, pair_table, hidden, w_down))
    grad_probs = slot_grads.reshape(-1)[bucket_pos].reshape(TOKENS, TOP)
    return grad_hidden, grad_down, grad_probs
```

```python
import functools

import jax
import jax.numpy as jnp
import numpy as np
from jax import lax
from jax.experimental import pallas as pl
from jax.experimental.pallas import tpu as pltpu
from jax.sharding import PartitionSpec as P

MIB = 1024 * 1024
CHUNKS = 2


def cycle_of(count):
    bits = count.bit_length() - 1
    if count != 1 << bits or count < 4:
        return list(range(count))
    width = 1 << (bits // 2)
    depth = count // width
    walk = [z * width for z in range(depth)]
    for turn, z in enumerate(reversed(range(depth))):
        columns = list(range(1, width))
        walk += [z * width + y for y in (columns if turn % 2 == 0 else columns[::-1])]
    return walk


def offsets_of(count, chunk):
    far = count // 2
    behind = far if chunk % 2 == 0 else count - 1 - far
    ahead = count - 1 - behind
    return [0] + [-k for k in range(1, behind + 1)] + [k for k in range(1, ahead + 1)]


def order_table(count, chunk):
    walk = cycle_of(count)
    place = {expert: at for at, expert in enumerate(walk)}
    offsets = offsets_of(count, chunk)
    return np.array(
        [[walk[(place[e] + o) % count] for o in offsets] for e in range(count)], np.int32
    )


def meta_kernel(experts, ids_ref, combine_ref, meta_ref):
    rows, picks = ids_ref.shape
    ids = ids_ref[...]
    weights = combine_ref[...].astype(jnp.float32)
    lane = lax.broadcasted_iota(jnp.int32, (rows, 128), 1)
    named = jnp.zeros((rows, 128), jnp.float32)
    prob = jnp.zeros((rows, 128), jnp.float32)
    for k in range(picks):
        hit = ids[:, k : k + 1] == lane
        named = jnp.where(hit, 1.0, named)
        prob = jnp.where(hit, weights[:, k : k + 1], prob)
    named_t = jnp.transpose(named)
    prob_t = jnp.transpose(prob)
    earlier = (
        lax.broadcasted_iota(jnp.int32, (rows, rows), 0)
        < lax.broadcasted_iota(jnp.int32, (rows, rows), 1)
    ).astype(jnp.bfloat16)
    before = jnp.dot(named_t.astype(jnp.bfloat16), earlier, preferred_element_type=jnp.float32)
    slot_t = jnp.where(named_t > 0.5, before, -1.0)
    both = jnp.concatenate([prob_t[:experts], slot_t[:experts]], axis=0).astype(jnp.bfloat16)
    meta_ref[...] = jnp.zeros_like(meta_ref)
    for group in range(2 * experts // 16):
        meta_ref[:, group * rows : (group + 1) * rows] = both[group * 16 : (group + 1) * 16]


def place_kernel(has_meta, count, cap, tokens, mine_ref, order_ref, *refs):
    blocks, refs = refs[:count], refs[count:]
    if has_meta:
        hidden_ref, placed_ref, part_ref, rows_ref, scaled_ref = refs
    else:
        rows_in, hidden_ref, placed_ref, part_ref, scaled_ref = refs
    expert = mine_ref[0]
    sub = lax.broadcasted_iota(jnp.int32, (16, tokens), 0)
    at = lax.broadcasted_iota(jnp.int32, (cap, tokens), 0).astype(jnp.float32)
    for i in range(count):
        source = order_ref[i]
        block = blocks[i]
        if has_meta:
            prob = jnp.zeros((1, tokens), jnp.float32)
            slot = jnp.zeros((1, tokens), jnp.float32)
            for group in range(2 * count // 16):
                piece = block[tokens : tokens + 16, group * tokens : (group + 1) * tokens].astype(
                    jnp.float32
                )
                row = sub + group * 16
                prob = prob + jnp.sum(jnp.where(row == expert, piece, 0.0), 0, keepdims=True)
                slot = slot + jnp.sum(
                    jnp.where(row == expert + count, piece, 0.0), 0, keepdims=True
                )
            rows_ref[pl.ds(source, 1), :] = jnp.concatenate([prob, slot], axis=1)
        else:
            both = rows_in[pl.ds(source, 1), :]
            prob, slot = both[:, :tokens], both[:, tokens:]
        hit = slot == at
        pick = jnp.where(hit, 1.0, 0.0).astype(jnp.bfloat16)
        weighted = jnp.where(hit, prob, 0.0).astype(jnp.bfloat16)
        grads = block[:tokens, :]
        start = pl.multiple_of(source * cap, cap)
        placed_ref[pl.ds(start, cap), :] = jnp.dot(
            pick, grads, preferred_element_type=jnp.float32
        ).astype(jnp.bfloat16)
        scaled_ref[pl.ds(start, cap), :] = jnp.dot(
            weighted, grads, preferred_element_type=jnp.float32
        ).astype(jnp.bfloat16)
    columns = scaled_ref.shape[1]
    step = min(256, columns)
    for c in range(columns // step):
        part_ref[c * step : (c + 1) * step, :] = lax.dot_general(
            scaled_ref[:, c * step : (c + 1) * step],
            hidden_ref[...],
            (((0,), (0,)), ((), ())),
            preferred_element_type=jnp.float32,
        ).astype(jnp.bfloat16)


def project_kernel(masks, count, cap, tokens, group, mine_ref, *refs):
    placed = refs[:CHUNKS]
    rows_ref, hidden_ref, w_ref, grad_ref, token_ref = refs[CHUNKS:]
    dp = mine_ref[1]
    pieces = len(masks)
    wide = placed[0].shape[1] // pieces
    per = wide * CHUNKS
    step = pl.program_id(0)
    acc = None
    for c in range(CHUNKS):
        for j, mask in enumerate(masks):
            start = pl.multiple_of((dp ^ mask) * per + c * wide, wide)
            term = jnp.dot(
                placed[c][:, j * wide : (j + 1) * wide],
                w_ref[pl.ds(start, wide), :],
                preferred_element_type=jnp.float32,
            )
            acc = term if acc is None else acc + term
    slot_grad = jnp.sum(acc * hidden_ref[...].astype(jnp.float32), axis=1, keepdims=True)
    at = lax.broadcasted_iota(jnp.int32, (cap, tokens), 0).astype(jnp.float32)
    for g in range(group):
        source = step * group + g
        both = rows_ref[pl.ds(source, 1), :]
        prob, slot = both[:, :tokens], both[:, tokens:]
        hit = slot == at
        column = jnp.sum(jnp.where(hit, prob, 0.0), axis=1, keepdims=True)
        grad_ref[g * cap : (g + 1) * cap, :] = (column * acc[g * cap : (g + 1) * cap]).astype(
            jnp.bfloat16
        )
        token_ref[pl.ds(source, 1), :] = jnp.sum(
            jnp.where(hit, slot_grad[g * cap : (g + 1) * cap], 0.0), axis=0, keepdims=True
        )


def body(replicas, out_grad, combine, expert_ids, hidden, w_down):
    tokens, width = out_grad.shape
    _, count, cap, inner = hidden.shape
    slots = count * cap
    mine = lax.axis_index("expert")
    dp = lax.axis_index("dp")
    where = jnp.stack([mine, dp]).astype(jnp.int32)
    hidden2 = hidden.reshape(slots, inner)
    weight = w_down.reshape(width, inner)
    wide = width // (replicas * CHUNKS)
    columns = wide * replicas
    bits = replicas.bit_length() - 1
    masks = sorted(range(replicas), key=lambda m: [-(m >> b & 1) for b in range(bits)])

    vmem = pl.BlockSpec(memory_space=pltpu.VMEM)
    smem = pl.BlockSpec(memory_space=pltpu.SMEM)
    meta = pl.pallas_call(
        functools.partial(meta_kernel, count),
        out_shape=jax.ShapeDtypeStruct((16, columns), jnp.bfloat16),
        in_specs=[vmem, vmem],
        out_specs=vmem,
    )(expert_ids, combine)

    def columns_of(chunk):
        return jnp.concatenate(
            [
                lax.dynamic_slice(
                    out_grad, (0, (dp ^ m) * wide * CHUNKS + chunk * wide), (tokens, wide)
                )
                for m in masks
            ],
            axis=1,
        )

    walk = cycle_of(count)
    forth = [(walk[i], walk[(i + 1) % count]) for i in range(count)]
    back = [(b, a) for a, b in forth]
    own = [columns_of(c) for c in range(CHUNKS)]
    own[0] = jnp.concatenate([own[0], meta], axis=0)
    held = []
    for chunk in range(CHUNKS):
        offsets = offsets_of(count, chunk)
        got = {0: own[chunk]}
        for o in offsets[1:]:
            if o < 0:
                got[o] = lax.ppermute(got[o + 1], "expert", forth)
            else:
                got[o] = lax.ppermute(got[o - 1], "expert", back)
        held.append([got[o] for o in offsets])

    placed, parts, rows = [], [], None
    for chunk in range(CHUNKS):
        order = jnp.asarray(order_table(count, chunk))[mine]
        first = chunk == 0
        shapes = [
            jax.ShapeDtypeStruct((slots, columns), jnp.bfloat16),
            jax.ShapeDtypeStruct((columns, inner), jnp.bfloat16),
        ]
        if first:
            shapes.append(jax.ShapeDtypeStruct((count, 2 * tokens), jnp.float32))
        results = pl.pallas_call(
            functools.partial(place_kernel, first, count, cap, tokens),
            out_shape=shapes,
            in_specs=[smem, smem] + [vmem] * (count + (1 if first else 2)),
            out_specs=[vmem] * len(shapes),
            scratch_shapes=[pltpu.VMEM((slots, columns), jnp.bfloat16)],
            compiler_params=pltpu.CompilerParams(vmem_limit_bytes=32 * MIB),
            cost_estimate=pl.CostEstimate(
                flops=2 * slots * columns * inner, bytes_accessed=8 * MIB, transcendentals=0
            ),
        )(where, order, *held[chunk], *([] if first else [rows]), hidden2)
        placed.append(results[0])
        parts.append(results[1])
        if first:
            rows = results[2]

    group = max(1, 256 // cap)
    block = group * cap
    grad_hidden, by_token = pl.pallas_call(
        functools.partial(project_kernel, masks, count, cap, tokens, group),
        grid=(slots // block,),
        out_shape=[
            jax.ShapeDtypeStruct((slots, inner), jnp.bfloat16),
            jax.ShapeDtypeStruct((count, tokens), jnp.float32),
        ],
        in_specs=[smem]
        + [pl.BlockSpec((block, columns), lambda i: (i, 0))] * CHUNKS
        + [
            pl.BlockSpec((count, 2 * tokens), lambda i: (0, 0)),
            pl.BlockSpec((block, inner), lambda i: (i, 0)),
            pl.BlockSpec((width, inner), lambda i: (0, 0), pipeline_mode=pl.Buffered(1)),
        ],
        out_specs=[
            pl.BlockSpec((block, inner), lambda i: (i, 0)),
            pl.BlockSpec((count, tokens), lambda i: (0, 0)),
        ],
        compiler_params=pltpu.CompilerParams(vmem_limit_bytes=32 * MIB),
        cost_estimate=pl.CostEstimate(
            flops=2 * slots * width * inner, bytes_accessed=16 * MIB, transcendentals=0
        ),
    )(where, *placed, rows, hidden2, weight)

    downs = []
    for chunk in range(CHUNKS):
        part = parts[chunk]
        for b in range(bits):
            half = part.shape[0] // 2
            arrived = lax.ppermute(
                part[:half], "dp", [(r, r ^ (1 << b)) for r in range(replicas)]
            )
            part = (part[half:].astype(jnp.float32) + arrived.astype(jnp.float32)).astype(
                jnp.bfloat16
            )
        downs.append(part)
    grad_down = jnp.concatenate(downs, axis=0)[None]

    returned = lax.all_to_all(by_token, "expert", split_axis=0, concat_axis=0, tiled=True)
    hit = expert_ids[:, :, None] == jnp.arange(count, dtype=jnp.int32)[None, None, :]
    grad_probs = jnp.sum(jnp.where(hit, returned.T[:, None, :], 0.0), axis=2)
    return grad_hidden.reshape(hidden.shape), grad_down, grad_probs


def solution(mesh):
    in_specs = (
        P(("dp", "expert"), None),
        P(("dp", "expert"), None),
        P(("dp", "expert"), None),
        P("expert", "dp", None, None),
        P("expert", None, None),
    )
    out_specs = (P("expert", "dp", None, None), P("expert", "dp", None), P(("dp", "expert"), None))
    return jax.shard_map(
        functools.partial(body, mesh.shape["dp"]),
        mesh=mesh,
        in_specs=in_specs,
        out_specs=out_specs,
        check_vma=False,
    )
```

```python
import functools

import jax
import jax.numpy as jnp
import numpy as np
from jax import lax
from jax.experimental import pallas as pl
from jax.experimental.pallas import tpu as pltpu
from jax.sharding import PartitionSpec as P

MIB = 1024 * 1024
CHUNKS = 2
CUTS = (12, 18, 26)


def cycle_of(count):
    bits = count.bit_length() - 1
    if count != 1 << bits or count < 4:
        return list(range(count))
    width = 1 << (bits // 2)
    depth = count // width
    walk = [z * width for z in range(depth)]
    for turn, z in enumerate(reversed(range(depth))):
        columns = list(range(1, width))
        walk += [z * width + y for y in (columns if turn % 2 == 0 else columns[::-1])]
    return walk


def offsets_of(count, chunk):
    far = count // 2
    behind = far - 1
    ahead = count - 2 - behind
    near = [-k for k in range(1, behind + 1)] + [k for k in range(1, ahead + 1)]
    return [0] + near + [-far if chunk % 2 == 0 else count - far]


def order_table(count, chunk):
    walk = cycle_of(count)
    place = {expert: at for at, expert in enumerate(walk)}
    offsets = offsets_of(count, chunk)
    return np.array(
        [[walk[(place[e] + o) % count] for o in offsets] for e in range(count)], np.int32
    )


def head_kernel(experts, masks, mine_ref, ids_ref, combine_ref, grad_ref, *own_refs):
    picks, rows = ids_ref.shape
    dp = mine_ref[1]
    columns = own_refs[0].shape[1]
    for c, own in enumerate(own_refs):
        wide = columns // len(masks[c])
        for j, mask in enumerate(masks[c]):
            start = pl.multiple_of((dp ^ mask) * wide, wide)
            own[:rows, j * wide : (j + 1) * wide] = grad_ref[:, pl.ds(start, wide)]
    ids = ids_ref[...]
    weights = combine_ref[...].astype(jnp.float32)
    line = lax.broadcasted_iota(jnp.int32, (experts, rows), 0)
    named = jnp.zeros((experts, rows), jnp.float32)
    prob = jnp.zeros((experts, rows), jnp.float32)
    for k in range(picks):
        hit = ids[k : k + 1, :] == line
        named = jnp.where(hit, 1.0, named)
        prob = jnp.where(hit, weights[k : k + 1, :], prob)
    earlier = (
        lax.broadcasted_iota(jnp.int32, (rows, rows), 0)
        < lax.broadcasted_iota(jnp.int32, (rows, rows), 1)
    ).astype(jnp.bfloat16)
    before = jnp.dot(named.astype(jnp.bfloat16), earlier, preferred_element_type=jnp.float32)
    slot = jnp.where(named > 0.5, before, -1.0)
    both = jnp.concatenate([prob, slot], axis=0).astype(jnp.bfloat16)
    groups = 2 * experts // 16
    for group in range(groups):
        own_refs[0][rows:, group * rows : (group + 1) * rows] = both[group * 16 : (group + 1) * 16]
    if groups * rows < columns:
        own_refs[0][rows:, groups * rows :] = jnp.zeros((16, columns - groups * rows), jnp.bfloat16)


def row_of(block, expert, count, tokens):
    sub = lax.broadcasted_iota(jnp.int32, (16, tokens), 0)
    prob = jnp.zeros((1, tokens), jnp.float32)
    slot = jnp.zeros((1, tokens), jnp.float32)
    for group in range(2 * count // 16):
        piece = block[tokens : tokens + 16, group * tokens : (group + 1) * tokens]
        piece = piece.astype(jnp.float32)
        row = sub + group * 16
        prob = prob + jnp.sum(jnp.where(row == expert, piece, 0.0), 0, keepdims=True)
        slot = slot + jnp.sum(jnp.where(row == expert + count, piece, 0.0), 0, keepdims=True)
    return jnp.concatenate([prob, slot], axis=1)


def weights_of(row, cap, tokens):
    at = lax.broadcasted_iota(jnp.int32, (cap, tokens), 0).astype(jnp.float32)
    return jnp.where(row[:, tokens:] == at, row[:, :tokens], 0.0).astype(jnp.bfloat16)


def product(left, right):
    return lax.dot_general(
        left, right, (((0,), (0,)), ((), ())), preferred_element_type=jnp.float32
    )


def early_kernel(at_order, count, cap, tokens, where_ref, *refs):
    blocks, refs = refs[: count - 1], refs[count - 1 :]
    hidden_ref, rows_ref, placed_ref, *sum_refs, scaled_ref = refs
    rows_ref[...] = jnp.zeros_like(rows_ref)
    for i in range(count):
        source = where_ref[at_order + i]
        here = pl.ds(pl.multiple_of(source * cap, cap), cap)
        if i == count - 1:
            scaled_ref[here, :] = jnp.zeros((cap, scaled_ref.shape[1]), jnp.bfloat16)
            continue
        row = row_of(blocks[i], where_ref[0], count, tokens)
        rows_ref[pl.ds(source, 1), :] = row
        spread(row, cap, tokens, blocks[i][:tokens, :], here, placed_ref, scaled_ref)
    wide = sum_refs[0].shape[0]
    for j, sum_ref in enumerate(sum_refs):
        sum_ref[...] = product(scaled_ref[:, j * wide : (j + 1) * wide], hidden_ref[...])


def spread(row, cap, tokens, grads, here, placed_ref, scaled_ref):
    at = lax.broadcasted_iota(jnp.int32, (cap, tokens), 0).astype(jnp.float32)
    hit = row[:, tokens:] == at
    for weight, out_ref in ((1.0, placed_ref), (row[:, :tokens], scaled_ref)):
        pick = jnp.where(hit, weight, 0.0).astype(jnp.bfloat16)
        out_ref[here, :] = jnp.dot(pick, grads, preferred_element_type=jnp.float32).astype(
            jnp.bfloat16
        )


def late_kernel(at_order, count, cap, tokens, where_ref, block_ref, near_ref, hidden_ref, *refs):
    *refs, rows_ref = refs
    source = where_ref[at_order + count - 1]
    row = row_of(block_ref, where_ref[0], count, tokens)
    rows_ref[...] = near_ref[...]
    rows_ref[pl.ds(source, 1), :] = row
    sum_refs, part_refs = refs[: len(refs) // 2], refs[len(refs) // 2 :]
    wide = sum_refs[0].shape[0]
    scaled = jnp.dot(
        weights_of(row, cap, tokens), block_ref[:tokens, :], preferred_element_type=jnp.float32
    ).astype(jnp.bfloat16)
    saved = hidden_ref[pl.ds(pl.multiple_of(source * cap, cap), cap), :]
    for j, (sum_ref, part_ref) in enumerate(zip(sum_refs, part_refs)):
        part_ref[...] = (
            sum_ref[...] + product(scaled[:, j * wide : (j + 1) * wide], saved)
        ).astype(jnp.bfloat16)


def part_kernel(scaled_ref, hidden_ref, *part_refs):
    wide = part_refs[0].shape[0]
    for j, part_ref in enumerate(part_refs):
        here = slice(j * wide, (j + 1) * wide)
        part_ref[...] = product(scaled_ref[:, here], hidden_ref[...]).astype(jnp.bfloat16)


def final_kernel(kept_ref, moved_ref, *refs):
    out_ref = refs[-1]
    low = 0
    for ref in refs[:-1]:
        here = slice(low, low + ref.shape[0])
        out_ref[here, :] = (
            kept_ref[here, :].astype(jnp.float32)
            + moved_ref[here, :].astype(jnp.float32)
            + ref[...].astype(jnp.float32)
        ).astype(out_ref.dtype)
        low += ref.shape[0]


def projected(rows, dp, masks, w_ref, wide):
    acc = None
    for j, mask in enumerate(masks):
        start = pl.multiple_of((dp ^ mask) * wide, wide)
        term = jnp.dot(
            rows[:, j * wide : (j + 1) * wide],
            w_ref[pl.ds(start, wide), :],
            preferred_element_type=jnp.float32,
        )
        acc = term if acc is None else acc + term
    return acc


def project_kernel(at_order, masks, count, cap, tokens, size, where_ref, block_ref, *refs):
    rows_ref, near_ref, w_ref, sum_ref, placed_ref = refs
    source = where_ref[at_order + count - 1]
    here = pl.ds(pl.multiple_of(source * cap, cap), cap)
    at = lax.broadcasted_iota(jnp.int32, (cap, tokens), 0).astype(jnp.float32)
    hit = rows_ref[pl.ds(source, 1), :][:, tokens:] == at
    placed_ref[...] = near_ref[...]
    placed_ref[here, :] = jnp.dot(
        jnp.where(hit, 1.0, 0.0).astype(jnp.bfloat16),
        block_ref[:tokens, :],
        preferred_element_type=jnp.float32,
    ).astype(jnp.bfloat16)
    wide = placed_ref.shape[1] // len(masks)

    def some(step, carry):
        here = pl.ds(pl.multiple_of(step * size, size), size)
        sum_ref[here, :] = projected(placed_ref[here, :], where_ref[1], masks, w_ref, wide)
        return carry

    lax.fori_loop(0, placed_ref.shape[0] // size, some, 0)


def finish(acc, row, cap, tokens, saved, grad_ref, here, token_ref, line):
    at = lax.broadcasted_iota(jnp.int32, (cap, tokens), 0).astype(jnp.float32)
    hit = row[:, tokens:] == at
    column = jnp.sum(jnp.where(hit, row[:, :tokens], 0.0), axis=1, keepdims=True)
    grad_ref[here, :] = (column * acc).astype(jnp.bfloat16)
    slot_grad = jnp.sum(acc * saved.astype(jnp.float32), axis=1, keepdims=True)
    token_ref[pl.ds(line, 1), :] = jnp.sum(
        jnp.where(hit, slot_grad, 0.0), axis=0, keepdims=True
    )


def finish_kernel(at_order, masks, count, cap, tokens, size, where_ref, *refs):
    blocks, refs = refs[:count], refs[count:]
    rows_ref, w_ref, before_ref, hidden_ref, grad_ref, token_ref, scaled_ref, placed_ref = refs
    wide = placed_ref.shape[1] // len(masks)
    for i in range(count):
        source = where_ref[at_order + i]
        here = pl.ds(pl.multiple_of(source * cap, cap), cap)
        row = rows_ref[pl.ds(source, 1), :]
        spread(row, cap, tokens, blocks[i][:tokens, :], here, placed_ref, scaled_ref)

    def some(step, carry):
        first = pl.multiple_of(step * size, size)
        here = pl.ds(first, size)
        acc = projected(placed_ref[here, :], where_ref[1], masks, w_ref, wide)
        acc = acc + before_ref[here, :]
        saved = hidden_ref[here, :]
        for g in range(size // cap):
            source = step * (size // cap) + g
            part = slice(g * cap, (g + 1) * cap)
            there = pl.ds(pl.multiple_of(first + g * cap, cap), cap)
            row = rows_ref[pl.ds(source, 1), :]
            line = source
            finish(acc[part], row, cap, tokens, saved[part], grad_ref, there, token_ref, line)
        return carry

    lax.fori_loop(0, placed_ref.shape[0] // size, some, 0)


def after(value, *others):
    return lax.optimization_barrier((value, *others))[0]


def body(replicas, out_grad, combine, expert_ids, hidden, w_down):
    tokens, width = out_grad.shape
    _, count, cap, inner = hidden.shape
    slots = count * cap
    mine = lax.axis_index("expert")
    dp = lax.axis_index("dp")
    where = jnp.stack([mine, dp]).astype(jnp.int32)
    hidden2 = hidden.reshape(slots, inner)
    weight = w_down.reshape(width, inner)
    columns = width // CHUNKS
    bits = replicas.bit_length() - 1
    top = replicas // 2
    masks = sorted(range(top), key=lambda m: [-(m >> b & 1) for b in range(bits)])
    masks = [[m | top for m in masks], masks]

    table = np.concatenate([order_table(count, c) for c in range(CHUNKS)], axis=1)
    table = np.array(
        [[e, r, *table[e]] for r in range(replicas) for e in range(count)], np.int32
    )
    places = lax.dynamic_slice(jnp.asarray(table), (dp * count + mine, 0), (1, table.shape[1]))[0]

    vmem = pl.BlockSpec(memory_space=pltpu.VMEM)
    smem = pl.BlockSpec(memory_space=pltpu.SMEM)
    anywhere = pl.BlockSpec(memory_space=pl.ANY)
    own = pl.pallas_call(
        functools.partial(head_kernel, count, masks),
        out_shape=[
            jax.ShapeDtypeStruct((tokens + (16 if c == 0 else 0), columns), jnp.bfloat16)
            for c in range(CHUNKS)
        ],
        grid=(1,),
        in_specs=[smem]
        + [
            pl.BlockSpec(v.shape, lambda i: (0, 0)) for v in (expert_ids.T, combine.T, out_grad)
        ],
        out_specs=[vmem] * CHUNKS,
        compiler_params=pltpu.CompilerParams(vmem_limit_bytes=8 * MIB),
    )(where, expert_ids.T, combine.T, out_grad)

    walk = cycle_of(count)
    forth = [(walk[i], walk[(i + 1) % count]) for i in range(count)]
    back = [(b, a) for a, b in forth]
    got = [{0: own[c]} for c in range(CHUNKS)]

    def step(chunk, k, *others):
        offsets = offsets_of(count, chunk)
        for sign, pairs in ((-1, forth), (1, back)):
            if sign * k in offsets:
                value = got[chunk][sign * (k - 1)]
                if others:
                    value = after(value, *others)
                got[chunk][sign * k] = lax.ppermute(value, "expert", pairs)

    wide = width // replicas

    def call(kernel, outs, args, scratch=(), limit=16, aliases=None):
        return pl.pallas_call(
            kernel,
            out_shape=[jax.ShapeDtypeStruct(*out) for out in outs],
            in_specs=[smem] + [vmem] * len(args),
            out_specs=[vmem] * len(outs),
            scratch_shapes=[pltpu.VMEM(*s) for s in scratch],
            input_output_aliases=aliases or {},
            compiler_params=pltpu.CompilerParams(vmem_limit_bytes=limit * MIB),
        )(places, *args)

    bf16, f32 = jnp.bfloat16, jnp.float32
    all_placed = ((slots, columns), bf16)
    piece = ((wide, inner), bf16)
    table = ((count, 2 * tokens), f32)
    size = max(1, 256 // cap) * cap

    def add(kept, arrived):
        return (kept.astype(jnp.float32) + arrived.astype(jnp.float32)).astype(jnp.bfloat16)

    def exchange(value, b):
        return lax.ppermute(value, "dp", [(r, r ^ (1 << b)) for r in range(replicas)])

    def reduced(parts, moved):
        for b in range(1, bits - 1):
            half = len(parts) // 2
            leaves = [add(k, a) for k, a in zip(parts[:half], moved[:half])]
            parts = [add(k, a) for k, a in zip(parts[half:], moved[half:])]
            moved = [exchange(v, b) for v in leaves]
        return parts[0], moved[0]

    far = count // 2
    at0, at1 = 2, 2 + count
    for k in range(1, far + 1):
        step(0, k, *([places] if k == 2 else []))
    step(1, 1, got[0][1 - far], got[0][far - 1])
    held = [got[0][o] for o in offsets_of(count, 0)]
    rows, placed, *sums = call(
        functools.partial(early_kernel, at0, count, cap, tokens),
        [table, all_placed] + [((wide, inner), f32)] * top,
        [*held[:-1], hidden2],
        [all_placed],
    )
    last = after(held[-1], got[1][-1], got[1][1])
    *parts, rows = call(
        functools.partial(late_kernel, at0, count, cap, tokens),
        [piece] * top + [table],
        [last, rows, hidden2, *sums],
    )
    moved = [exchange(p, 0) for p in parts[: top // 2]]
    parts = parts[top // 2 :]
    leaves = add(*reduced(parts, moved))
    cuts = [0, *(wide * c // 32 for c in CUTS), wide]

    def leave(n, *others):
        piece = leaves[cuts[n] : cuts[n + 1]]
        return exchange(after(piece, *others) if others else piece, bits - 1)

    for k in range(2, far - 1):
        step(1, k, *([got[1][1 - k], got[1][k - 1]] if k > 2 else []))
    arrived = [leave(0)]
    ready = (got[1][2 - far], got[1][far - 2], leaves)
    step(1, far - 1, *ready)
    acc = call(
        functools.partial(project_kernel, at0, masks[0], count, cap, tokens, size),
        [((slots, inner), f32)],
        [after(last, *ready), rows, placed, weight],
        [all_placed],
    )[0]
    ready = (got[1][1 - far], got[1][far - 1], acc, arrived[0])
    step(1, far, *ready)
    arrived.append(leave(1, *ready))
    held = [got[1][o] for o in offsets_of(count, 1)]
    ready = (held[-1], arrived[1])
    arrived.append(leave(2, *ready))
    grad_hidden, by_token, scaled = call(
        functools.partial(finish_kernel, at1, masks[1], count, cap, tokens, size),
        [((slots, inner), bf16), ((count, tokens), f32), all_placed],
        [after(held[0], *ready), *held[1:], rows, weight, acc, hidden2],
        [all_placed],
        limit=20,
    )
    ready = (arrived[2], by_token)
    arrived.append(leave(3, *ready))
    scaled = after(scaled, *ready)

    parts = pl.pallas_call(
        part_kernel,
        out_shape=[jax.ShapeDtypeStruct(*piece)] * top,
        in_specs=[vmem] * 2,
        out_specs=[vmem] * top,
        compiler_params=pltpu.CompilerParams(vmem_limit_bytes=16 * MIB),
    )(scaled, hidden2)
    moved = [exchange(p, 0) for p in parts[: top // 2]]
    kept, moved = reduced(parts[top // 2 :], moved)
    grad_down = pl.pallas_call(
        final_kernel,
        out_shape=jax.ShapeDtypeStruct((wide, inner), jnp.bfloat16),
        in_specs=[vmem] * (2 + len(arrived)),
        out_specs=vmem,
        compiler_params=pltpu.CompilerParams(vmem_limit_bytes=16 * MIB),
    )(kept, moved, *arrived)[None]

    returned = lax.all_to_all(by_token, "expert", split_axis=0, concat_axis=0, tiled=True)
    hit = expert_ids[:, :, None] == jnp.arange(count, dtype=jnp.int32)[None, None, :]
    grad_probs = jnp.sum(jnp.where(hit, returned.T[:, None, :], 0.0), axis=2)
    return grad_hidden.reshape(hidden.shape), grad_down, grad_probs


def solution(mesh):
    in_specs = (
        P(("dp", "expert"), None),
        P(("dp", "expert"), None),
        P(("dp", "expert"), None),
        P("expert", "dp", None, None),
        P("expert", None, None),
    )
    out_specs = (P("expert", "dp", None, None), P("expert", "dp", None), P(("dp", "expert"), None))
    return jax.shard_map(
        functools.partial(body, mesh.shape["dp"]),
        mesh=mesh,
        in_specs=in_specs,
        out_specs=out_specs,
        check_vma=False,
    )
```

```python
import functools

import jax
import jax.numpy as jnp
import numpy as np
from jax import lax
from jax.experimental import pallas as pl
from jax.experimental.pallas import tpu as pltpu
from jax.sharding import PartitionSpec as P

MIB = 1024 * 1024
CHUNKS = 2
CUTS = (11, 19)
LAG = 2


def cycle_of(count):
    bits = count.bit_length() - 1
    if count != 1 << bits or count < 4:
        return list(range(count))
    width = 1 << (bits // 2)
    depth = count // width
    walk = [z * width for z in range(depth)]
    for turn, z in enumerate(reversed(range(depth))):
        columns = list(range(1, width))
        walk += [z * width + y for y in (columns if turn % 2 == 0 else columns[::-1])]
    return walk


def offsets_of(count, chunk):
    far = count // 2
    behind = far - 1
    ahead = count - 2 - behind
    near = [-k for k in range(1, behind + 1)] + [k for k in range(1, ahead + 1)]
    return [0] + near + [-far if chunk % 2 == 0 else count - far]


def order_table(count, chunk):
    walk = cycle_of(count)
    place = {expert: at for at, expert in enumerate(walk)}
    offsets = offsets_of(count, chunk)
    return np.array(
        [[walk[(place[e] + o) % count] for o in offsets] for e in range(count)], np.int32
    )


def head_kernel(experts, masks, ids_ref, combine_ref, grad_ref, *own_refs):
    picks, rows = ids_ref.shape
    dp = lax.axis_index("dp")
    columns = own_refs[0].shape[1]
    for c, own in enumerate(own_refs):
        wide = columns // len(masks[c])
        for j, mask in enumerate(masks[c]):
            start = pl.multiple_of((dp ^ mask) * wide, wide)
            own[:rows, j * wide : (j + 1) * wide] = grad_ref[:, pl.ds(start, wide)]
    ids = ids_ref[...]
    weights = combine_ref[...].astype(jnp.float32)
    line = lax.broadcasted_iota(jnp.int32, (experts, rows), 0)
    named = jnp.zeros((experts, rows), jnp.float32)
    prob = jnp.zeros((experts, rows), jnp.float32)
    for k in range(picks):
        hit = ids[k : k + 1, :] == line
        named = jnp.where(hit, 1.0, named)
        prob = jnp.where(hit, weights[k : k + 1, :], prob)
    earlier = (
        lax.broadcasted_iota(jnp.int32, (rows, rows), 0)
        < lax.broadcasted_iota(jnp.int32, (rows, rows), 1)
    ).astype(jnp.bfloat16)
    before = jnp.dot(named.astype(jnp.bfloat16), earlier, preferred_element_type=jnp.float32)
    slot = jnp.where(named > 0.5, before, -1.0)
    both = jnp.concatenate([prob, slot], axis=0).astype(jnp.bfloat16)
    groups = 2 * experts // 16
    for group in range(groups):
        own_refs[0][rows:, group * rows : (group + 1) * rows] = both[group * 16 : (group + 1) * 16]
    if groups * rows < columns:
        own_refs[0][rows:, groups * rows :] = jnp.zeros((16, columns - groups * rows), jnp.bfloat16)


def row_of(block, expert, count, tokens):
    sub = lax.broadcasted_iota(jnp.int32, (16, tokens), 0)
    prob = jnp.zeros((1, tokens), jnp.float32)
    slot = jnp.zeros((1, tokens), jnp.float32)
    for group in range(2 * count // 16):
        piece = block[tokens : tokens + 16, group * tokens : (group + 1) * tokens]
        piece = piece.astype(jnp.float32)
        row = sub + group * 16
        prob = prob + jnp.sum(jnp.where(row == expert, piece, 0.0), 0, keepdims=True)
        slot = slot + jnp.sum(jnp.where(row == expert + count, piece, 0.0), 0, keepdims=True)
    return jnp.concatenate([prob, slot], axis=1)


def weights_of(row, cap, tokens):
    at = lax.broadcasted_iota(jnp.int32, (cap, tokens), 0).astype(jnp.float32)
    return jnp.where(row[:, tokens:] == at, row[:, :tokens], 0.0).astype(jnp.bfloat16)


def product(left, right):
    return lax.dot_general(
        left, right, (((0,), (0,)), ((), ())), preferred_element_type=jnp.float32
    )


def early_kernel(at_order, count, cap, tokens, where_ref, *refs):
    blocks, refs = refs[: count - 1], refs[count - 1 :]
    hidden_ref, rows_ref, placed_ref, *sum_refs, scaled_ref = refs
    rows_ref[...] = jnp.zeros_like(rows_ref)
    for i in range(count):
        source = where_ref[at_order + i]
        here = pl.ds(pl.multiple_of(source * cap, cap), cap)
        if i == count - 1:
            scaled_ref[here, :] = jnp.zeros((cap, scaled_ref.shape[1]), jnp.bfloat16)
            continue
        row = row_of(blocks[i], where_ref[0], count, tokens)
        rows_ref[pl.ds(source, 1), :] = row
        spread(row, cap, tokens, blocks[i][:tokens, :], here, placed_ref, scaled_ref)
    wide = sum_refs[0].shape[0]
    for j, sum_ref in enumerate(sum_refs):
        sum_ref[...] = product(scaled_ref[:, j * wide : (j + 1) * wide], hidden_ref[...])


def spread(row, cap, tokens, grads, here, placed_ref, scaled_ref):
    at = lax.broadcasted_iota(jnp.int32, (cap, tokens), 0).astype(jnp.float32)
    hit = row[:, tokens:] == at
    picks = jnp.concatenate(
        [jnp.where(hit, weight, 0.0).astype(jnp.bfloat16) for weight in (1.0, row[:, :tokens])]
    )
    both = jnp.dot(picks, grads, preferred_element_type=jnp.float32).astype(jnp.bfloat16)
    placed_ref[here, :] = both[:cap]
    scaled_ref[here, :] = both[cap:]


def late_kernel(at_order, count, cap, tokens, where_ref, block_ref, near_ref, hidden_ref, *refs):
    *refs, rows_ref = refs
    source = where_ref[at_order + count - 1]
    row = row_of(block_ref, where_ref[0], count, tokens)
    rows_ref[...] = near_ref[...]
    rows_ref[pl.ds(source, 1), :] = row
    sum_refs, part_refs = refs[: len(refs) // 2], refs[len(refs) // 2 :]
    wide = sum_refs[0].shape[0]
    scaled = jnp.dot(
        weights_of(row, cap, tokens), block_ref[:tokens, :], preferred_element_type=jnp.float32
    ).astype(jnp.bfloat16)
    saved = hidden_ref[pl.ds(pl.multiple_of(source * cap, cap), cap), :]
    for j, (sum_ref, part_ref) in enumerate(zip(sum_refs, part_refs)):
        part_ref[...] = (
            sum_ref[...] + product(scaled[:, j * wide : (j + 1) * wide], saved)
        ).astype(jnp.bfloat16)


def part_kernel(low, scaled_ref, hidden_ref, *refs):
    part_refs = refs if low == 0 else refs[1:]
    wide = part_refs[0].shape[0]
    for j, part_ref in enumerate(part_refs):
        here = slice(low + j * wide, low + (j + 1) * wide)
        part_ref[...] = product(scaled_ref[:, here], hidden_ref[...]).astype(jnp.bfloat16)


def final_kernel(kept_ref, moved_ref, *refs):
    out_ref = refs[-1]
    low = 0
    for ref in refs[:-1]:
        here = slice(low, low + ref.shape[0])
        out_ref[here, :] = (
            kept_ref[here, :].astype(jnp.float32)
            + moved_ref[here, :].astype(jnp.float32)
            + ref[...].astype(jnp.float32)
        ).astype(out_ref.dtype)
        low += ref.shape[0]


def projected(rows, dp, masks, w_ref, wide):
    acc = None
    for j, mask in enumerate(masks):
        start = pl.multiple_of((dp ^ mask) * wide, wide)
        term = jnp.dot(
            rows[:, j * wide : (j + 1) * wide],
            w_ref[pl.ds(start, wide), :],
            preferred_element_type=jnp.float32,
        )
        acc = term if acc is None else acc + term
    return acc


def project_kernel(at_order, masks, count, cap, tokens, size, where_ref, block_ref, *refs):
    rows_ref, near_ref, w_ref, sum_ref, placed_ref = refs
    source = where_ref[at_order + count - 1]
    here = pl.ds(pl.multiple_of(source * cap, cap), cap)
    at = lax.broadcasted_iota(jnp.int32, (cap, tokens), 0).astype(jnp.float32)
    hit = rows_ref[pl.ds(source, 1), :][:, tokens:] == at
    placed_ref[...] = near_ref[...]
    placed_ref[here, :] = jnp.dot(
        jnp.where(hit, 1.0, 0.0).astype(jnp.bfloat16),
        block_ref[:tokens, :],
        preferred_element_type=jnp.float32,
    ).astype(jnp.bfloat16)
    wide = placed_ref.shape[1] // len(masks)

    def some(step, carry):
        here = pl.ds(pl.multiple_of(step * size, size), size)
        sum_ref[here, :] = projected(placed_ref[here, :], where_ref[1], masks, w_ref, wide)
        return carry

    lax.fori_loop(0, placed_ref.shape[0] // size, some, 0)


def finish(acc, row, cap, tokens, saved, grad_ref, here, token_ref, line):
    at = lax.broadcasted_iota(jnp.int32, (cap, tokens), 0).astype(jnp.float32)
    hit = row[:, tokens:] == at
    column = jnp.sum(jnp.where(hit, row[:, :tokens], 0.0), axis=1, keepdims=True)
    grad_ref[here, :] = (column * acc).astype(jnp.bfloat16)
    slot_grad = jnp.sum(acc * saved.astype(jnp.float32), axis=1, keepdims=True)
    token_ref[pl.ds(line, 1), :] = jnp.sum(
        jnp.where(hit, slot_grad, 0.0), axis=0, keepdims=True
    )


def finish_kernel(at_order, masks, count, cap, tokens, size, where_ref, *refs):
    blocks, refs = refs[:count], refs[count:]
    rows_ref, w_ref, before_ref, hidden_ref, grad_ref, token_ref, scaled_ref, placed_ref = refs
    wide = placed_ref.shape[1] // len(masks)
    for i in range(count):
        source = where_ref[at_order + i]
        here = pl.ds(pl.multiple_of(source * cap, cap), cap)
        row = rows_ref[pl.ds(source, 1), :]
        spread(row, cap, tokens, blocks[i][:tokens, :], here, placed_ref, scaled_ref)

    def some(step, carry):
        first = pl.multiple_of(step * size, size)
        here = pl.ds(first, size)
        acc = projected(placed_ref[here, :], where_ref[1], masks, w_ref, wide)
        acc = acc + before_ref[here, :]
        saved = hidden_ref[here, :]
        for g in range(size // cap):
            source = step * (size // cap) + g
            part = slice(g * cap, (g + 1) * cap)
            there = pl.ds(pl.multiple_of(first + g * cap, cap), cap)
            row = rows_ref[pl.ds(source, 1), :]
            finish(acc[part], row, cap, tokens, saved[part], grad_ref, there, token_ref, source)
        return carry

    lax.fori_loop(0, placed_ref.shape[0] // size, some, 0)


def after(value, *others):
    return lax.optimization_barrier((value, *others))[0]


def body(replicas, out_grad, combine, expert_ids, hidden, w_down):
    tokens, width = out_grad.shape
    _, count, cap, inner = hidden.shape
    slots = count * cap
    mine = lax.axis_index("expert")
    dp = lax.axis_index("dp")
    hidden2 = hidden.reshape(slots, inner)
    weight = w_down.reshape(width, inner)
    columns = width // CHUNKS
    bits = replicas.bit_length() - 1
    top = replicas // 2
    masks = sorted(range(top), key=lambda m: [-(m >> b & 1) for b in range(bits)])
    masks = [[m | top for m in masks], masks]

    table = np.concatenate([order_table(count, c) for c in range(CHUNKS)], axis=1)
    table = np.array(
        [[e, r, *table[e]] for r in range(replicas) for e in range(count)], np.int32
    )
    places = lax.dynamic_slice(jnp.asarray(table), (dp * count + mine, 0), (1, table.shape[1]))[0]

    vmem = pl.BlockSpec(memory_space=pltpu.VMEM)
    smem = pl.BlockSpec(memory_space=pltpu.SMEM)
    anywhere = pl.BlockSpec(memory_space=pl.ANY)
    own = pl.pallas_call(
        functools.partial(head_kernel, count, masks),
        out_shape=[
            jax.ShapeDtypeStruct((tokens + (16 if c == 0 else 0), columns), jnp.bfloat16)
            for c in range(CHUNKS)
        ],
        grid=(1,),
        in_specs=[
            pl.BlockSpec(v.shape, lambda i: (0, 0)) for v in (expert_ids.T, combine.T, out_grad)
        ],
        out_specs=[vmem] * CHUNKS,
        compiler_params=pltpu.CompilerParams(vmem_limit_bytes=56 * MIB),
    )(expert_ids.T, combine.T, out_grad)

    walk = cycle_of(count)
    forth = [(walk[i], walk[(i + 1) % count]) for i in range(count)]
    back = [(b, a) for a, b in forth]
    got = [{0: own[c]} for c in range(CHUNKS)]

    def step(chunk, k, *others):
        offsets = offsets_of(count, chunk)
        for sign, pairs in ((-1, forth), (1, back)):
            if sign * k in offsets:
                value = got[chunk][sign * (k - 1)]
                if others:
                    value = after(value, *others)
                got[chunk][sign * k] = lax.ppermute(value, "expert", pairs)

    wide = width // replicas

    def call(kernel, outs, args, scratch=(), limit=16, aliases=None):
        return pl.pallas_call(
            kernel,
            out_shape=[jax.ShapeDtypeStruct(*out) for out in outs],
            in_specs=[smem] + [vmem] * len(args),
            out_specs=[vmem] * len(outs),
            scratch_shapes=[pltpu.VMEM(*s) for s in scratch],
            input_output_aliases=aliases or {},
            compiler_params=pltpu.CompilerParams(vmem_limit_bytes=limit * MIB),
        )(places, *args)

    bf16, f32 = jnp.bfloat16, jnp.float32
    all_placed = ((slots, columns), bf16)
    piece = ((wide, inner), bf16)
    table = ((count, 2 * tokens), f32)
    size = max(1, 256 // cap) * cap

    def add(kept, arrived):
        return (kept.astype(jnp.float32) + arrived.astype(jnp.float32)).astype(jnp.bfloat16)

    def exchange(value, b):
        return lax.ppermute(value, "dp", [(r, r ^ (1 << b)) for r in range(replicas)])

    def reduced(parts, moved):
        for b in range(1, bits - 1):
            half = len(parts) // 2
            leaves = [add(k, a) for k, a in zip(parts[:half], moved[:half])]
            parts = [add(k, a) for k, a in zip(parts[half:], moved[half:])]
            moved = [exchange(v, b) for v in leaves]
        return parts[0], moved[0]

    far = count // 2
    at0, at1 = 2, 2 + count
    ready = ()
    for k in range(1, far + 1):
        ready = (places,) if k == 2 else ready
        step(0, k, *ready)
        if k > LAG:
            step(1, k - LAG, *ready)
            ready = [got[1][o] for o in (LAG - k, k - LAG)]
        if k >= LAG and k < far:
            ready = [*(ready if k > LAG else ()), got[0][-k], got[0][k]]
    held = [got[0][o] for o in offsets_of(count, 0)]
    rows, placed, *sums = call(
        functools.partial(early_kernel, at0, count, cap, tokens),
        [table, all_placed] + [((wide, inner), f32)] * top,
        [*held[:-1], hidden2],
        [all_placed],
    )
    ready = (held[-1], got[1][LAG - far], got[1][far - LAG])
    for k in range(far - LAG + 1, far):
        step(1, k, *(ready if k == far - LAG + 1 else ()))
    last = after(*ready)
    *parts, rows = call(
        functools.partial(late_kernel, at0, count, cap, tokens),
        [piece] * top + [table],
        [last, rows, hidden2, *sums],
    )
    moved = [exchange(p, 0) for p in parts[: top // 2]]
    parts = parts[top // 2 :]
    leaves = add(*reduced(parts, moved))
    cuts = [0, *(wide * c // 32 for c in CUTS), wide]

    def leave(n, *others):
        piece = leaves[cuts[n] : cuts[n + 1]]
        return exchange(after(piece, *others) if others else piece, bits - 1)

    arrived = [leave(0)]
    ready = (got[1][1 - far], got[1][far - 1], leaves)
    step(1, far, *ready)
    acc = call(
        functools.partial(project_kernel, at0, masks[0], count, cap, tokens, size),
        [((slots, inner), f32)],
        [after(last, *ready), rows, placed, weight],
        [all_placed],
    )[0]
    held = [got[1][o] for o in offsets_of(count, 1)]
    ready = (held[-1], arrived[0], acc)
    arrived.append(leave(1, *ready))
    grad_hidden, by_token, scaled = call(
        functools.partial(finish_kernel, at1, masks[1], count, cap, tokens, size),
        [((slots, inner), bf16), ((count, tokens), f32), all_placed],
        [after(held[0], *ready), *held[1:], rows, weight, acc, hidden2],
        [all_placed],
        limit=20,
    )
    ready = (arrived[1], by_token)
    arrived.append(leave(2, *ready))
    returned = lax.all_to_all(by_token, "expert", split_axis=0, concat_axis=0, tiled=True)
    scaled = after(scaled, *ready)

    def part_of(low, *others):
        return pl.pallas_call(
            functools.partial(part_kernel, low),
            out_shape=[jax.ShapeDtypeStruct(*piece)] * (top // 2),
            in_specs=[vmem] * (2 + len(others)),
            out_specs=[vmem] * (top // 2),
            compiler_params=pltpu.CompilerParams(vmem_limit_bytes=16 * MIB),
        )(scaled, hidden2, *others)

    moved = [exchange(p, 0) for p in part_of(0)]
    kept, moved = reduced(part_of(columns // 2, returned), moved)
    grad_down = pl.pallas_call(
        final_kernel,
        out_shape=jax.ShapeDtypeStruct((wide, inner), jnp.bfloat16),
        in_specs=[vmem] * (2 + len(arrived)),
        out_specs=vmem,
        compiler_params=pltpu.CompilerParams(vmem_limit_bytes=16 * MIB),
    )(kept, moved, *arrived)[None]

    hit = expert_ids[:, :, None] == jnp.arange(count, dtype=jnp.int32)[None, None, :]
    grad_probs = jnp.sum(jnp.where(hit, returned.T[:, None, :], 0.0), axis=2)
    return grad_hidden.reshape(hidden.shape), grad_down, grad_probs


def solution(mesh):
    in_specs = (
        P(("dp", "expert"), None),
        P(("dp", "expert"), None),
        P(("dp", "expert"), None),
        P("expert", "dp", None, None),
        P("expert", None, None),
    )
    out_specs = (P("expert", "dp", None, None), P("expert", "dp", None), P(("dp", "expert"), None))
    return jax.shard_map(
        functools.partial(body, mesh.shape["dp"]),
        mesh=mesh,
        in_specs=in_specs,
        out_specs=out_specs,
        check_vma=False,
    )
```

```python
import functools

import jax
import jax.numpy as jnp
import numpy as np
from jax import lax
from jax.experimental import pallas as pl
from jax.experimental.pallas import tpu as pltpu
from jax.sharding import PartitionSpec as P

MIB = 1024 * 1024
CHUNKS = 2
CUTS = (11, 19)
LAG = 2


def cycle_of(count):
    bits = count.bit_length() - 1
    if count != 1 << bits or count < 4:
        return list(range(count))
    width = 1 << (bits // 2)
    depth = count // width
    walk = [z * width for z in range(depth)]
    for turn, z in enumerate(reversed(range(depth))):
        columns = list(range(1, width))
        walk += [z * width + y for y in (columns if turn % 2 == 0 else columns[::-1])]
    return walk


def offsets_of(count, chunk):
    far = count // 2
    behind = far - 1
    ahead = count - 2 - behind
    near = [-k for k in range(1, behind + 1)] + [k for k in range(1, ahead + 1)]
    return [0] + near + [-far if chunk % 2 == 0 else count - far]


def order_table(count, chunk):
    walk = cycle_of(count)
    place = {expert: at for at, expert in enumerate(walk)}
    offsets = offsets_of(count, chunk)
    return np.array(
        [[walk[(place[e] + o) % count] for o in offsets] for e in range(count)], np.int32
    )


def head_kernel(experts, masks, ids_ref, combine_ref, grad_ref, *own_refs):
    picks, rows = ids_ref.shape
    dp = lax.axis_index("dp")
    columns = own_refs[0].shape[1]
    for c, own in enumerate(own_refs):
        wide = columns // len(masks[c])
        for j, mask in enumerate(masks[c]):
            start = pl.multiple_of((dp ^ mask) * wide, wide)
            own[:rows, j * wide : (j + 1) * wide] = grad_ref[:, pl.ds(start, wide)]
    ids = ids_ref[...]
    weights = combine_ref[...].astype(jnp.float32)
    line = lax.broadcasted_iota(jnp.int32, (experts, rows), 0)
    named = jnp.zeros((experts, rows), jnp.float32)
    prob = jnp.zeros((experts, rows), jnp.float32)
    for k in range(picks):
        hit = ids[k : k + 1, :] == line
        named = jnp.where(hit, 1.0, named)
        prob = jnp.where(hit, weights[k : k + 1, :], prob)
    earlier = (
        lax.broadcasted_iota(jnp.int32, (rows, rows), 0)
        < lax.broadcasted_iota(jnp.int32, (rows, rows), 1)
    ).astype(jnp.bfloat16)
    before = jnp.dot(named.astype(jnp.bfloat16), earlier, preferred_element_type=jnp.float32)
    slot = jnp.where(named > 0.5, before, -1.0)
    both = jnp.concatenate([prob, slot], axis=0).astype(jnp.bfloat16)
    groups = 2 * experts // 16
    for group in range(groups):
        own_refs[0][rows:, group * rows : (group + 1) * rows] = both[group * 16 : (group + 1) * 16]
    if groups * rows < columns:
        own_refs[0][rows:, groups * rows :] = jnp.zeros((16, columns - groups * rows), jnp.bfloat16)


def row_of(block, expert, count, tokens):
    sub = lax.broadcasted_iota(jnp.int32, (16, tokens), 0)
    prob = jnp.zeros((1, tokens), jnp.float32)
    slot = jnp.zeros((1, tokens), jnp.float32)
    for group in range(2 * count // 16):
        piece = block[tokens : tokens + 16, group * tokens : (group + 1) * tokens]
        piece = piece.astype(jnp.float32)
        row = sub + group * 16
        prob = prob + jnp.sum(jnp.where(row == expert, piece, 0.0), 0, keepdims=True)
        slot = slot + jnp.sum(jnp.where(row == expert + count, piece, 0.0), 0, keepdims=True)
    return jnp.concatenate([prob, slot], axis=1)


def weights_of(row, cap, tokens):
    at = lax.broadcasted_iota(jnp.int32, (cap, tokens), 0).astype(jnp.float32)
    return jnp.where(row[:, tokens:] == at, row[:, :tokens], 0.0).astype(jnp.bfloat16)


def product(left, right):
    return lax.dot_general(
        left, right, (((0,), (0,)), ((), ())), preferred_element_type=jnp.float32
    )


def early_kernel(at_order, count, cap, tokens, where_ref, *refs):
    blocks, refs = refs[: count - 1], refs[count - 1 :]
    hidden_ref, rows_ref, placed_ref, *sum_refs, scaled_ref = refs
    rows_ref[...] = jnp.zeros_like(rows_ref)
    for i in range(count):
        source = where_ref[at_order + i]
        here = pl.ds(pl.multiple_of(source * cap, cap), cap)
        if i == count - 1:
            scaled_ref[here, :] = jnp.zeros((cap, scaled_ref.shape[1]), jnp.bfloat16)
            continue
        row = row_of(blocks[i], where_ref[0], count, tokens)
        rows_ref[pl.ds(source, 1), :] = row
        spread(row, cap, tokens, blocks[i][:tokens, :], here, placed_ref, scaled_ref)
    wide = sum_refs[0].shape[0]
    for j, sum_ref in enumerate(sum_refs):
        sum_ref[...] = product(scaled_ref[:, j * wide : (j + 1) * wide], hidden_ref[...])


def spread(row, cap, tokens, grads, here, placed_ref, scaled_ref):
    at = lax.broadcasted_iota(jnp.int32, (cap, tokens), 0).astype(jnp.float32)
    hit = row[:, tokens:] == at
    picks = jnp.concatenate(
        [jnp.where(hit, weight, 0.0).astype(jnp.bfloat16) for weight in (1.0, row[:, :tokens])]
    )
    both = jnp.dot(picks, grads, preferred_element_type=jnp.float32).astype(jnp.bfloat16)
    placed_ref[here, :] = both[:cap]
    scaled_ref[here, :] = both[cap:]


def late_kernel(at_order, count, cap, tokens, where_ref, block_ref, near_ref, hidden_ref, *refs):
    *refs, rows_ref = refs
    source = where_ref[at_order + count - 1]
    row = row_of(block_ref, where_ref[0], count, tokens)
    rows_ref[...] = near_ref[...]
    rows_ref[pl.ds(source, 1), :] = row
    sum_refs, part_refs = refs[: len(refs) // 2], refs[len(refs) // 2 :]
    wide = sum_refs[0].shape[0]
    scaled = jnp.dot(
        weights_of(row, cap, tokens), block_ref[:tokens, :], preferred_element_type=jnp.float32
    ).astype(jnp.bfloat16)
    saved = hidden_ref[pl.ds(pl.multiple_of(source * cap, cap), cap), :]
    for j, (sum_ref, part_ref) in enumerate(zip(sum_refs, part_refs)):
        part_ref[...] = (
            sum_ref[...] + product(scaled[:, j * wide : (j + 1) * wide], saved)
        ).astype(jnp.bfloat16)


def part_kernel(low, scaled_ref, hidden_ref, *part_refs):
    wide = part_refs[0].shape[0]
    for j, part_ref in enumerate(part_refs):
        here = slice(low + j * wide, low + (j + 1) * wide)
        part_ref[...] = product(scaled_ref[:, here], hidden_ref[...]).astype(jnp.bfloat16)


def final_kernel(kept_ref, moved_ref, *refs):
    out_ref = refs[-1]
    low = 0
    for ref in refs[:-1]:
        here = slice(low, low + ref.shape[0])
        out_ref[here, :] = (
            kept_ref[here, :].astype(jnp.float32)
            + moved_ref[here, :].astype(jnp.float32)
            + ref[...].astype(jnp.float32)
        ).astype(out_ref.dtype)
        low += ref.shape[0]


def projected(rows, dp, masks, w_ref, wide):
    acc = None
    for j, mask in enumerate(masks):
        start = pl.multiple_of((dp ^ mask) * wide, wide)
        term = jnp.dot(
            rows[:, j * wide : (j + 1) * wide],
            w_ref[pl.ds(start, wide), :],
            preferred_element_type=jnp.float32,
        )
        acc = term if acc is None else acc + term
    return acc


def project_kernel(at_order, masks, count, cap, tokens, size, where_ref, block_ref, *refs):
    rows_ref, near_ref, w_ref, sum_ref, placed_ref = refs
    source = where_ref[at_order + count - 1]
    here = pl.ds(pl.multiple_of(source * cap, cap), cap)
    at = lax.broadcasted_iota(jnp.int32, (cap, tokens), 0).astype(jnp.float32)
    hit = rows_ref[pl.ds(source, 1), :][:, tokens:] == at
    placed_ref[...] = near_ref[...]
    placed_ref[here, :] = jnp.dot(
        jnp.where(hit, 1.0, 0.0).astype(jnp.bfloat16),
        block_ref[:tokens, :],
        preferred_element_type=jnp.float32,
    ).astype(jnp.bfloat16)
    wide = placed_ref.shape[1] // len(masks)

    def some(step, carry):
        here = pl.ds(pl.multiple_of(step * size, size), size)
        sum_ref[here, :] = projected(placed_ref[here, :], where_ref[1], masks, w_ref, wide)
        return carry

    lax.fori_loop(0, placed_ref.shape[0] // size, some, 0, unroll=True)


def finish(acc, row, cap, tokens, saved, grad_ref, here, token_ref, line):
    at = lax.broadcasted_iota(jnp.int32, (cap, tokens), 0).astype(jnp.float32)
    hit = row[:, tokens:] == at
    column = jnp.sum(jnp.where(hit, row[:, :tokens], 0.0), axis=1, keepdims=True)
    grad_ref[here, :] = (column * acc).astype(jnp.bfloat16)
    slot_grad = jnp.sum(acc * saved.astype(jnp.float32), axis=1, keepdims=True)
    token_ref[pl.ds(line, 1), :] = jnp.sum(
        jnp.where(hit, slot_grad, 0.0), axis=0, keepdims=True
    )


def finish_kernel(at_order, masks, count, cap, tokens, size, where_ref, *refs):
    blocks, refs = refs[:count], refs[count:]
    rows_ref, w_ref, before_ref, hidden_ref, grad_ref, token_ref, scaled_ref, placed_ref = refs
    wide = placed_ref.shape[1] // len(masks)
    for i in range(count):
        source = where_ref[at_order + i]
        here = pl.ds(pl.multiple_of(source * cap, cap), cap)
        row = rows_ref[pl.ds(source, 1), :]
        spread(row, cap, tokens, blocks[i][:tokens, :], here, placed_ref, scaled_ref)

    def some(step, carry):
        first = pl.multiple_of(step * size, size)
        here = pl.ds(first, size)
        acc = projected(placed_ref[here, :], where_ref[1], masks, w_ref, wide)
        acc = acc + before_ref[here, :]
        saved = hidden_ref[here, :]
        for g in range(size // cap):
            source = step * (size // cap) + g
            part = slice(g * cap, (g + 1) * cap)
            there = pl.ds(pl.multiple_of(first + g * cap, cap), cap)
            row = rows_ref[pl.ds(source, 1), :]
            finish(acc[part], row, cap, tokens, saved[part], grad_ref, there, token_ref, source)
        return carry

    lax.fori_loop(0, placed_ref.shape[0] // size, some, 0, unroll=True)


def after(value, *others):
    return lax.optimization_barrier((value, *others))[0]


def body(replicas, out_grad, combine, expert_ids, hidden, w_down):
    tokens, width = out_grad.shape
    _, count, cap, inner = hidden.shape
    slots = count * cap
    mine = lax.axis_index("expert")
    dp = lax.axis_index("dp")
    hidden2 = hidden.reshape(slots, inner)
    weight = w_down.reshape(width, inner)
    columns = width // CHUNKS
    bits = replicas.bit_length() - 1
    top = replicas // 2
    masks = sorted(range(top), key=lambda m: [-(m >> b & 1) for b in range(bits)])
    masks = [[m | top for m in masks], masks]

    table = np.concatenate([order_table(count, c) for c in range(CHUNKS)], axis=1)
    table = np.array(
        [[e, r, *table[e]] for r in range(replicas) for e in range(count)], np.int32
    )
    places = lax.dynamic_slice(jnp.asarray(table), (dp * count + mine, 0), (1, table.shape[1]))[0]

    vmem = pl.BlockSpec(memory_space=pltpu.VMEM)
    smem = pl.BlockSpec(memory_space=pltpu.SMEM)
    anywhere = pl.BlockSpec(memory_space=pl.ANY)
    own = pl.pallas_call(
        functools.partial(head_kernel, count, masks),
        out_shape=[
            jax.ShapeDtypeStruct((tokens + (16 if c == 0 else 0), columns), jnp.bfloat16)
            for c in range(CHUNKS)
        ],
        grid=(1,),
        in_specs=[
            pl.BlockSpec(v.shape, lambda i: (0, 0)) for v in (expert_ids.T, combine.T, out_grad)
        ],
        out_specs=[vmem] * CHUNKS,
        compiler_params=pltpu.CompilerParams(vmem_limit_bytes=56 * MIB),
    )(expert_ids.T, combine.T, out_grad)

    walk = cycle_of(count)
    forth = [(walk[i], walk[(i + 1) % count]) for i in range(count)]
    back = [(b, a) for a, b in forth]
    got = [{0: own[c]} for c in range(CHUNKS)]

    def step(chunk, k, *others):
        offsets = offsets_of(count, chunk)
        for sign, pairs in ((-1, forth), (1, back)):
            if sign * k in offsets:
                value = got[chunk][sign * (k - 1)]
                if others:
                    value = after(value, *others)
                got[chunk][sign * k] = lax.ppermute(value, "expert", pairs)

    wide = width // replicas

    def call(kernel, outs, args, scratch=(), limit=16, aliases=None):
        return pl.pallas_call(
            kernel,
            out_shape=[jax.ShapeDtypeStruct(*out) for out in outs],
            in_specs=[smem] + [vmem] * len(args),
            out_specs=[vmem] * len(outs),
            scratch_shapes=[pltpu.VMEM(*s) for s in scratch],
            input_output_aliases=aliases or {},
            compiler_params=pltpu.CompilerParams(vmem_limit_bytes=limit * MIB),
        )(places, *args)

    bf16, f32 = jnp.bfloat16, jnp.float32
    all_placed = ((slots, columns), bf16)
    piece = ((wide, inner), bf16)
    table = ((count, 2 * tokens), f32)
    size = max(1, 256 // cap) * cap

    def add(kept, arrived):
        return (kept.astype(jnp.float32) + arrived.astype(jnp.float32)).astype(jnp.bfloat16)

    def exchange(value, b):
        return lax.ppermute(value, "dp", [(r, r ^ (1 << b)) for r in range(replicas)])

    def reduced(parts, moved):
        for b in range(1, bits - 1):
            half = len(parts) // 2
            leaves = [add(k, a) for k, a in zip(parts[:half], moved[:half])]
            parts = [add(k, a) for k, a in zip(parts[half:], moved[half:])]
            moved = [exchange(v, b) for v in leaves]
        return parts[0], moved[0]

    far = count // 2
    at0, at1 = 2, 2 + count
    ready = ()
    for k in range(1, far + 1):
        ready = (places,) if k == 2 else ready
        step(0, k, *ready)
        if k > LAG:
            step(1, k - LAG, *ready)
            ready = [got[1][o] for o in (LAG - k, k - LAG)]
        if k >= LAG and k < far:
            ready = [*(ready if k > LAG else ()), got[0][-k], got[0][k]]
    held = [got[0][o] for o in offsets_of(count, 0)]
    rows, placed, *sums = call(
        functools.partial(early_kernel, at0, count, cap, tokens),
        [table, all_placed] + [((wide, inner), f32)] * top,
        [*held[:-1], hidden2],
        [all_placed],
    )
    ready = (held[-1], got[1][LAG - far], got[1][far - LAG])
    for k in range(far - LAG + 1, far):
        step(1, k, *(ready if k == far - LAG + 1 else ()))
    last = after(*ready)
    *parts, rows = call(
        functools.partial(late_kernel, at0, count, cap, tokens),
        [piece] * top + [table],
        [last, rows, hidden2, *sums],
    )
    moved = [exchange(p, 0) for p in parts[: top // 2]]
    parts = parts[top // 2 :]
    leaves = add(*reduced(parts, moved))
    cuts = [0, *(wide * c // 32 for c in CUTS), wide]

    def leave(n, *others):
        piece = leaves[cuts[n] : cuts[n + 1]]
        return exchange(after(piece, *others) if others else piece, bits - 1)

    arrived = [leave(0)]
    ready = (got[1][1 - far], got[1][far - 1], leaves)
    step(1, far, *ready)
    acc = call(
        functools.partial(project_kernel, at0, masks[0], count, cap, tokens, size),
        [((slots, inner), f32)],
        [after(last, *ready), rows, placed, weight],
        [all_placed],
    )[0]
    held = [got[1][o] for o in offsets_of(count, 1)]
    ready = (held[-1], arrived[0], acc)
    arrived.append(leave(1, *ready))
    grad_hidden, by_token, scaled = call(
        functools.partial(finish_kernel, at1, masks[1], count, cap, tokens, size),
        [((slots, inner), bf16), ((count, tokens), f32), all_placed],
        [after(held[0], *ready), *held[1:], rows, weight, acc, hidden2],
        [all_placed],
        limit=20,
    )
    ready = (arrived[1], by_token)
    arrived.append(leave(2, *ready))
    returned = lax.all_to_all(by_token, "expert", split_axis=0, concat_axis=0, tiled=True)
    scaled = after(scaled, *ready)

    def part_of(low):
        return pl.pallas_call(
            functools.partial(part_kernel, low),
            out_shape=[jax.ShapeDtypeStruct(*piece)] * (top // 2),
            in_specs=[vmem] * 2,
            out_specs=[vmem] * (top // 2),
            compiler_params=pltpu.CompilerParams(vmem_limit_bytes=16 * MIB),
        )(scaled, hidden2)

    moved = [exchange(p, 0) for p in part_of(0)]
    kept, moved = reduced(part_of(columns // 2), moved)
    grad_down = pl.pallas_call(
        final_kernel,
        out_shape=jax.ShapeDtypeStruct((wide, inner), jnp.bfloat16),
        in_specs=[vmem] * (2 + len(arrived)),
        out_specs=vmem,
        compiler_params=pltpu.CompilerParams(vmem_limit_bytes=16 * MIB),
    )(kept, moved, *arrived)[None]

    hit = expert_ids[:, :, None] == jnp.arange(count, dtype=jnp.int32)[None, None, :]
    grad_probs = jnp.sum(jnp.where(hit, returned.T[:, None, :], 0.0), axis=2)
    return grad_hidden.reshape(hidden.shape), grad_down, grad_probs


def solution(mesh):
    in_specs = (
        P(("dp", "expert"), None),
        P(("dp", "expert"), None),
        P(("dp", "expert"), None),
        P("expert", "dp", None, None),
        P("expert", None, None),
    )
    out_specs = (P("expert", "dp", None, None), P("expert", "dp", None), P(("dp", "expert"), None))
    return jax.shard_map(
        functools.partial(body, mesh.shape["dp"]),
        mesh=mesh,
        in_specs=in_specs,
        out_specs=out_specs,
        check_vma=False,
    )
```

```python
import functools

import jax
import jax.numpy as jnp
import numpy as np
from jax import lax
from jax.experimental import pallas as pl
from jax.experimental.pallas import tpu as pltpu
from jax.sharding import PartitionSpec as P

MIB = 1024 * 1024
CHUNKS = 2
CUTS = (11, 19)
LAG = 2


def cycle_of(count):
    bits = count.bit_length() - 1
    if count != 1 << bits or count < 4:
        return list(range(count))
    width = 1 << (bits // 2)
    depth = count // width
    walk = [z * width for z in range(depth)]
    for turn, z in enumerate(reversed(range(depth))):
        columns = list(range(1, width))
        walk += [z * width + y for y in (columns if turn % 2 == 0 else columns[::-1])]
    return walk


def offsets_of(count, chunk):
    far = count // 2
    behind = far - 1
    ahead = count - 2 - behind
    near = [-k for k in range(1, behind + 1)] + [k for k in range(1, ahead + 1)]
    return [0] + near + [-far if chunk % 2 == 0 else count - far]


def order_table(count, chunk):
    walk = cycle_of(count)
    place = {expert: at for at, expert in enumerate(walk)}
    offsets = offsets_of(count, chunk)
    return np.array(
        [[walk[(place[e] + o) % count] for o in offsets] for e in range(count)], np.int32
    )


def head_kernel(experts, masks, ids_ref, combine_ref, grad_ref, *own_refs):
    picks, rows = ids_ref.shape
    dp = lax.axis_index("dp")
    columns = own_refs[0].shape[1]
    for c, own in enumerate(own_refs):
        wide = columns // len(masks[c])
        for j, mask in enumerate(masks[c]):
            start = pl.multiple_of((dp ^ mask) * wide, wide)
            own[:rows, j * wide : (j + 1) * wide] = grad_ref[:, pl.ds(start, wide)]
    ids = ids_ref[...]
    weights = combine_ref[...].astype(jnp.float32)
    line = lax.broadcasted_iota(jnp.int32, (experts, rows), 0)
    named = jnp.zeros((experts, rows), jnp.float32)
    prob = jnp.zeros((experts, rows), jnp.float32)
    for k in range(picks):
        hit = ids[k : k + 1, :] == line
        named = jnp.where(hit, 1.0, named)
        prob = jnp.where(hit, weights[k : k + 1, :], prob)
    earlier = (
        lax.broadcasted_iota(jnp.int32, (rows, rows), 0)
        < lax.broadcasted_iota(jnp.int32, (rows, rows), 1)
    ).astype(jnp.bfloat16)
    before = jnp.dot(named.astype(jnp.bfloat16), earlier, preferred_element_type=jnp.float32)
    slot = jnp.where(named > 0.5, before, -1.0)
    own_refs[0][rows:, :] = jnp.zeros((8, columns), jnp.bfloat16)
    for group in range(experts // 8):
        both = [v[group * 8 : (group + 1) * 8] for v in (prob, slot)]
        own_refs[0][rows:, 2 * group * rows : 2 * (group + 1) * rows] = jnp.concatenate(
            both, axis=1
        ).astype(jnp.bfloat16)


def row_of(block, expert, count, tokens):
    sub = lax.broadcasted_iota(jnp.int32, (8, 2 * tokens), 0)
    found = jnp.zeros((1, 2 * tokens), jnp.float32)
    for group in range(count // 8):
        piece = block[tokens : tokens + 8, 2 * group * tokens : 2 * (group + 1) * tokens]
        own = jnp.where(sub + group * 8 == expert, piece.astype(jnp.float32), 0.0)
        found = found + jnp.sum(own, 0, keepdims=True)
    return found


def weights_of(row, cap, tokens):
    at = lax.broadcasted_iota(jnp.int32, (cap, tokens), 0).astype(jnp.float32)
    return jnp.where(row[:, tokens:] == at, row[:, :tokens], 0.0).astype(jnp.bfloat16)


def product(left, right):
    return lax.dot_general(
        left, right, (((0,), (0,)), ((), ())), preferred_element_type=jnp.float32
    )


def early_kernel(at_order, count, cap, tokens, where_ref, *refs):
    blocks, refs = refs[: count - 1], refs[count - 1 :]
    hidden_ref, rows_ref, placed_ref, *sum_refs, scaled_ref = refs
    rows_ref[...] = jnp.zeros_like(rows_ref)
    for i in range(count):
        source = where_ref[at_order + i]
        here = pl.ds(pl.multiple_of(source * cap, cap), cap)
        if i == count - 1:
            scaled_ref[here, :] = jnp.zeros((cap, scaled_ref.shape[1]), jnp.bfloat16)
            continue
        row = row_of(blocks[i], where_ref[0], count, tokens)
        rows_ref[pl.ds(source, 1), :] = row
        spread(row, cap, tokens, blocks[i][:tokens, :], here, placed_ref, scaled_ref)
    wide = sum_refs[0].shape[0]
    for j, sum_ref in enumerate(sum_refs):
        sum_ref[...] = product(scaled_ref[:, j * wide : (j + 1) * wide], hidden_ref[...])


def spread(row, cap, tokens, grads, here, placed_ref, scaled_ref):
    at = lax.broadcasted_iota(jnp.int32, (cap, tokens), 0).astype(jnp.float32)
    hit = row[:, tokens:] == at
    picks = jnp.concatenate(
        [jnp.where(hit, weight, 0.0).astype(jnp.bfloat16) for weight in (1.0, row[:, :tokens])]
    )
    both = jnp.dot(picks, grads, preferred_element_type=jnp.float32).astype(jnp.bfloat16)
    placed_ref[here, :] = both[:cap]
    scaled_ref[here, :] = both[cap:]


def late_kernel(at_order, count, cap, tokens, where_ref, block_ref, near_ref, hidden_ref, *refs):
    *refs, rows_ref = refs
    source = where_ref[at_order + count - 1]
    row = row_of(block_ref, where_ref[0], count, tokens)
    rows_ref[...] = near_ref[...]
    rows_ref[pl.ds(source, 1), :] = row
    sum_refs, part_refs = refs[: len(refs) // 2], refs[len(refs) // 2 :]
    wide = sum_refs[0].shape[0]
    scaled = jnp.dot(
        weights_of(row, cap, tokens), block_ref[:tokens, :], preferred_element_type=jnp.float32
    ).astype(jnp.bfloat16)
    saved = hidden_ref[pl.ds(pl.multiple_of(source * cap, cap), cap), :]
    for j, (sum_ref, part_ref) in enumerate(zip(sum_refs, part_refs)):
        part_ref[...] = (
            sum_ref[...] + product(scaled[:, j * wide : (j + 1) * wide], saved)
        ).astype(jnp.bfloat16)


def part_kernel(low, scaled_ref, hidden_ref, *part_refs):
    wide = part_refs[0].shape[0]
    for j, part_ref in enumerate(part_refs):
        here = slice(low + j * wide, low + (j + 1) * wide)
        part_ref[...] = product(scaled_ref[:, here], hidden_ref[...]).astype(jnp.bfloat16)


def final_kernel(kept_ref, moved_ref, *refs):
    out_ref = refs[-1]
    low = 0
    for ref in refs[:-1]:
        here = slice(low, low + ref.shape[0])
        out_ref[here, :] = (
            kept_ref[here, :].astype(jnp.float32)
            + moved_ref[here, :].astype(jnp.float32)
            + ref[...].astype(jnp.float32)
        ).astype(out_ref.dtype)
        low += ref.shape[0]


def projected(rows, dp, masks, w_ref, wide):
    acc = None
    for j, mask in enumerate(masks):
        start = pl.multiple_of((dp ^ mask) * wide, wide)
        term = jnp.dot(
            rows[:, j * wide : (j + 1) * wide],
            w_ref[pl.ds(start, wide), :],
            preferred_element_type=jnp.float32,
        )
        acc = term if acc is None else acc + term
    return acc


def project_kernel(at_order, masks, count, cap, tokens, size, where_ref, block_ref, *refs):
    rows_ref, near_ref, w_ref, sum_ref, placed_ref = refs
    source = where_ref[at_order + count - 1]
    here = pl.ds(pl.multiple_of(source * cap, cap), cap)
    at = lax.broadcasted_iota(jnp.int32, (cap, tokens), 0).astype(jnp.float32)
    hit = rows_ref[pl.ds(source, 1), :][:, tokens:] == at
    placed_ref[...] = near_ref[...]
    placed_ref[here, :] = jnp.dot(
        jnp.where(hit, 1.0, 0.0).astype(jnp.bfloat16),
        block_ref[:tokens, :],
        preferred_element_type=jnp.float32,
    ).astype(jnp.bfloat16)
    wide = placed_ref.shape[1] // len(masks)

    def some(step, carry):
        here = pl.ds(pl.multiple_of(step * size, size), size)
        sum_ref[here, :] = projected(placed_ref[here, :], where_ref[1], masks, w_ref, wide)
        return carry

    lax.fori_loop(0, placed_ref.shape[0] // size, some, 0, unroll=True)


def finish(acc, row, cap, tokens, saved, grad_ref, here, token_ref, line):
    at = lax.broadcasted_iota(jnp.int32, (cap, tokens), 0).astype(jnp.float32)
    hit = row[:, tokens:] == at
    column = jnp.sum(jnp.where(hit, row[:, :tokens], 0.0), axis=1, keepdims=True)
    grad_ref[here, :] = (column * acc).astype(jnp.bfloat16)
    slot_grad = jnp.sum(acc * saved.astype(jnp.float32), axis=1, keepdims=True)
    token_ref[pl.ds(line, 1), :] = jnp.sum(
        jnp.where(hit, slot_grad, 0.0), axis=0, keepdims=True
    )


def finish_kernel(at_order, masks, count, cap, tokens, size, where_ref, *refs):
    blocks, refs = refs[:count], refs[count:]
    rows_ref, w_ref, before_ref, hidden_ref, grad_ref, token_ref, scaled_ref, placed_ref = refs
    wide = placed_ref.shape[1] // len(masks)
    for i in range(count):
        source = where_ref[at_order + i]
        here = pl.ds(pl.multiple_of(source * cap, cap), cap)
        row = rows_ref[pl.ds(source, 1), :]
        spread(row, cap, tokens, blocks[i][:tokens, :], here, placed_ref, scaled_ref)

    def some(step, carry):
        first = pl.multiple_of(step * size, size)
        here = pl.ds(first, size)
        acc = projected(placed_ref[here, :], where_ref[1], masks, w_ref, wide)
        acc = acc + before_ref[here, :]
        saved = hidden_ref[here, :]
        for g in range(size // cap):
            source = step * (size // cap) + g
            part = slice(g * cap, (g + 1) * cap)
            there = pl.ds(pl.multiple_of(first + g * cap, cap), cap)
            row = rows_ref[pl.ds(source, 1), :]
            finish(acc[part], row, cap, tokens, saved[part], grad_ref, there, token_ref, source)
        return carry

    lax.fori_loop(0, placed_ref.shape[0] // size, some, 0, unroll=True)


def after(value, *others):
    return lax.optimization_barrier((value, *others))[0]


def body(replicas, out_grad, combine, expert_ids, hidden, w_down):
    tokens, width = out_grad.shape
    _, count, cap, inner = hidden.shape
    slots = count * cap
    mine = lax.axis_index("expert")
    dp = lax.axis_index("dp")
    hidden2 = hidden.reshape(slots, inner)
    weight = w_down.reshape(width, inner)
    columns = width // CHUNKS
    bits = replicas.bit_length() - 1
    top = replicas // 2
    masks = sorted(range(top), key=lambda m: [-(m >> b & 1) for b in range(bits)])
    masks = [[m | top for m in masks], masks]

    table = np.concatenate([order_table(count, c) for c in range(CHUNKS)], axis=1)
    table = np.array(
        [[e, r, *table[e]] for r in range(replicas) for e in range(count)], np.int32
    )
    places = lax.dynamic_slice(jnp.asarray(table), (dp * count + mine, 0), (1, table.shape[1]))[0]

    vmem = pl.BlockSpec(memory_space=pltpu.VMEM)
    smem = pl.BlockSpec(memory_space=pltpu.SMEM)
    anywhere = pl.BlockSpec(memory_space=pl.ANY)
    own = pl.pallas_call(
        functools.partial(head_kernel, count, masks),
        out_shape=[
            jax.ShapeDtypeStruct((tokens + (8 if c == 0 else 0), columns), jnp.bfloat16)
            for c in range(CHUNKS)
        ],
        grid=(1,),
        in_specs=[
            pl.BlockSpec(v.shape, lambda i: (0, 0)) for v in (expert_ids.T, combine.T, out_grad)
        ],
        out_specs=[vmem] * CHUNKS,
        compiler_params=pltpu.CompilerParams(vmem_limit_bytes=56 * MIB),
    )(expert_ids.T, combine.T, out_grad)

    walk = cycle_of(count)
    forth = [(walk[i], walk[(i + 1) % count]) for i in range(count)]
    back = [(b, a) for a, b in forth]
    got = [{0: own[c]} for c in range(CHUNKS)]

    def step(chunk, k, *others):
        offsets = offsets_of(count, chunk)
        for sign, pairs in ((-1, forth), (1, back)):
            if sign * k in offsets:
                value = got[chunk][sign * (k - 1)]
                if others:
                    value = after(value, *others)
                got[chunk][sign * k] = lax.ppermute(value, "expert", pairs)

    wide = width // replicas

    def call(kernel, outs, args, scratch=(), limit=16, aliases=None):
        return pl.pallas_call(
            kernel,
            out_shape=[jax.ShapeDtypeStruct(*out) for out in outs],
            in_specs=[smem] + [vmem] * len(args),
            out_specs=[vmem] * len(outs),
            scratch_shapes=[pltpu.VMEM(*s) for s in scratch],
            input_output_aliases=aliases or {},
            compiler_params=pltpu.CompilerParams(vmem_limit_bytes=limit * MIB),
        )(places, *args)

    bf16, f32 = jnp.bfloat16, jnp.float32
    all_placed = ((slots, columns), bf16)
    piece = ((wide, inner), bf16)
    table = ((count, 2 * tokens), f32)
    size = max(1, 256 // cap) * cap

    def add(kept, arrived):
        return (kept.astype(jnp.float32) + arrived.astype(jnp.float32)).astype(jnp.bfloat16)

    def exchange(value, b):
        return lax.ppermute(value, "dp", [(r, r ^ (1 << b)) for r in range(replicas)])

    def reduced(parts, moved):
        for b in range(1, bits - 1):
            half = len(parts) // 2
            leaves = [add(k, a) for k, a in zip(parts[:half], moved[:half])]
            parts = [add(k, a) for k, a in zip(parts[half:], moved[half:])]
            moved = [exchange(v, b) for v in leaves]
        return parts[0], moved[0]

    far = count // 2
    at0, at1 = 2, 2 + count
    ready = ()
    for k in range(1, far + 1):
        ready = (places,) if k == 2 else ready
        step(0, k, *ready)
        if k > LAG:
            step(1, k - LAG, *ready)
            ready = [got[1][o] for o in (LAG - k, k - LAG)]
        if k >= LAG and k < far:
            ready = [*(ready if k > LAG else ()), got[0][-k], got[0][k]]
    held = [got[0][o] for o in offsets_of(count, 0)]
    rows, placed, *sums = call(
        functools.partial(early_kernel, at0, count, cap, tokens),
        [table, all_placed] + [((wide, inner), f32)] * top,
        [*held[:-1], hidden2],
        [all_placed],
    )
    ready = (held[-1], got[1][LAG - far], got[1][far - LAG])
    for k in range(far - LAG + 1, far):
        step(1, k, *(ready if k == far - LAG + 1 else ()))
    last = after(*ready)
    *parts, rows = call(
        functools.partial(late_kernel, at0, count, cap, tokens),
        [piece] * top + [table],
        [last, rows, hidden2, *sums],
    )
    moved = [exchange(p, 0) for p in parts[: top // 2]]
    parts = parts[top // 2 :]
    leaves = add(*reduced(parts, moved))
    cuts = [0, *(wide * c // 32 for c in CUTS), wide]

    def leave(n, *others):
        piece = leaves[cuts[n] : cuts[n + 1]]
        return exchange(after(piece, *others) if others else piece, bits - 1)

    arrived = [leave(0)]
    ready = (got[1][1 - far], got[1][far - 1], leaves)
    step(1, far, *ready)
    acc = call(
        functools.partial(project_kernel, at0, masks[0], count, cap, tokens, size),
        [((slots, inner), f32)],
        [after(last, *ready), rows, placed, weight],
        [all_placed],
    )[0]
    held = [got[1][o] for o in offsets_of(count, 1)]
    ready = (held[-1], arrived[0], acc)
    arrived.append(leave(1, *ready))
    grad_hidden, by_token, scaled = call(
        functools.partial(finish_kernel, at1, masks[1], count, cap, tokens, size),
        [((slots, inner), bf16), ((count, tokens), f32), all_placed],
        [after(held[0], *ready), *held[1:], rows, weight, acc, hidden2],
        [all_placed],
        limit=20,
    )
    ready = (arrived[1], by_token)
    arrived.append(leave(2, *ready))
    returned = lax.all_to_all(by_token, "expert", split_axis=0, concat_axis=0, tiled=True)
    scaled = after(scaled, *ready)

    def part_of(low):
        return pl.pallas_call(
            functools.partial(part_kernel, low),
            out_shape=[jax.ShapeDtypeStruct(*piece)] * (top // 2),
            in_specs=[vmem] * 2,
            out_specs=[vmem] * (top // 2),
            compiler_params=pltpu.CompilerParams(vmem_limit_bytes=16 * MIB),
        )(scaled, hidden2)

    moved = [exchange(p, 0) for p in part_of(0)]
    kept, moved = reduced(part_of(columns // 2), moved)
    grad_down = pl.pallas_call(
        final_kernel,
        out_shape=jax.ShapeDtypeStruct((wide, inner), jnp.bfloat16),
        in_specs=[vmem] * (2 + len(arrived)),
        out_specs=vmem,
        compiler_params=pltpu.CompilerParams(vmem_limit_bytes=16 * MIB),
    )(kept, moved, *arrived)[None]

    hit = expert_ids[:, :, None] == jnp.arange(count, dtype=jnp.int32)[None, None, :]
    grad_probs = jnp.sum(jnp.where(hit, returned.T[:, None, :], 0.0), axis=2)
    return grad_hidden.reshape(hidden.shape), grad_down, grad_probs


def solution(mesh):
    in_specs = (
        P(("dp", "expert"), None),
        P(("dp", "expert"), None),
        P(("dp", "expert"), None),
        P("expert", "dp", None, None),
        P("expert", None, None),
    )
    out_specs = (P("expert", "dp", None, None), P("expert", "dp", None), P(("dp", "expert"), None))
    return jax.shard_map(
        functools.partial(body, mesh.shape["dp"]),
        mesh=mesh,
        in_specs=in_specs,
        out_specs=out_specs,
        check_vma=False,
    )
```
